512 devices in a mesh: ctx: 64 (over z, y), ch: 8 (over x, core).
Axes of the slice: x: 4, y: 4, z: 16, core: 2. Of those that a mesh axis runs over, the one named last changes fastest.
Arguments:
- query_gate: bfloat16 [8192, 8192], P('ctx', 'ch'), may hold values from -6 to 6
- key_gate: bfloat16 [8192, 8192], P('ctx', 'ch'), may hold values from -6 to 6
- value_branch: bfloat16 [8192, 8192], P('ctx', 'ch'), may hold values from -6 to 6
- grad_out: bfloat16 [8192, 8192], P('ctx', 'ch'), may hold values from -0.625 to 0.625
- filters: float32 [512, 8192], P('ch', 'ctx'), may hold values from -2 to 2
- skip_bias: float32 [8192], P('ch'), may hold values from -2 to 2
Outputs:
- grad_query: bfloat16 [8192, 8192], P('ctx', 'ch')
- grad_key: bfloat16 [8192, 8192], P('ctx', 'ch')
- grad_value: bfloat16 [8192, 8192], P('ctx', 'ch')
- grad_filters: float32 [512, 8192], P('ch', 'ctx')
- grad_bias: float32 [8192], P('ch')
The draws below stay inside these ranges and needn't reach their ends.
All inputs are finite; a program needn't handle non-finite values.
Results may differ from the reference program's by a relative error of at most 0.0057.
Values may be sent and summed in bfloat16 or wider, within the bound.
No kernel may reach another device: no remote copies, remote signals or barrier semaphores. Data moves between devices by JAX's collectives and lax.ppermute only.
A program may use at most 64 MiB of HBM per device.

```python
import math
import jax
import jax.numpy as jnp
from jax import lax

D = 8192
FILTER_GROUPS = 512
TOKEN_COUNT = 8192


def draw_filters(key, part):
    key = jax.random.fold_in(key, 11)
    falloff_key, pulse_key, noise_key, scale_seed_key = jax.random.split(key, 4)
    delay_index = jnp.arange(TOKEN_COUNT, dtype=jnp.float32)[None, :]
    falloff_rates = jnp.exp(jax.random.uniform(falloff_key, (FILTER_GROUPS, 1), jnp.float32, math.log(0.3 / TOKEN_COUNT), math.log(1.0 / 30.0)))
    noise_component = jax.random.uniform(noise_key, (FILTER_GROUPS, TOKEN_COUNT), jnp.float32, -2.5, 2.5)
    token_positions = jax.random.randint(pulse_key, (FILTER_GROUPS, 3), 0, TOKEN_COUNT)
    pulse_train = jnp.ones((FILTER_GROUPS, TOKEN_COUNT), jnp.float32)
    for pulse_index in range(3):
        pulse_location = token_positions[:, pulse_index:pulse_index + 1].astype(jnp.float32)
        pulse_train = pulse_train * jnp.where(delay_index >= pulse_location, 0.6, 1.0)
    reach = jnp.minimum(float(TOKEN_COUNT), 0.5 / falloff_rates)
    filter_magnitude = jax.random.uniform(scale_seed_key, (FILTER_GROUPS, 1), jnp.float32, 1.0, 2.0) / jnp.sqrt(reach)
    return filter_magnitude * jnp.exp(-falloff_rates * delay_index) * pulse_train * noise_component


def level_of(rng, shape, shards, low, largest):
    loudness, own = 1.0, jax.random.fold_in(rng, 6)
    for dim, parts in shards:
        heights = jnp.exp(jax.random.uniform(jax.random.fold_in(own, dim), (parts,), jnp.float32, low / len(shards), largest / len(shards)))
        loudness = loudness * jnp.repeat(heights, shape[dim] // parts).reshape([-1 if axis == dim else 1 for axis in range(len(shape))])
    return loudness


def scatter_about(own_key, dims, spread, limit, pieces=(), kind=jnp.bfloat16):
    array = spread * jax.random.normal(own_key, dims, jnp.float32)
    if pieces:
        array = array * level_of(own_key, dims, pieces, -0.22, 0.18)
    return jnp.clip(array, -limit, limit).astype(kind)


def setup_inputs(seed: int = 0) -> dict:
    splits = jax.random.split(jax.random.key(seed), 7)
    query_gate = scatter_about(splits[0], (TOKEN_COUNT, D), 1.0, 6.0, ((0, 64), (1, 8)))
    key_gate = scatter_about(splits[1], (TOKEN_COUNT, D), 1.0, 6.0, ((0, 64), (1, 8)))
    value_branch = scatter_about(splits[2], (TOKEN_COUNT, D), 1.0, 6.0, ((0, 64), (1, 8)))
    grad_out = scatter_about(splits[3], (TOKEN_COUNT, D), 0.1, 0.625, ((0, 64), (1, 8)))
    filters = draw_filters(jax.random.fold_in(splits[6], 71), 0)
    skip_bias = jnp.clip(jax.random.uniform(splits[5], (D,), jnp.float32, -2.0, 2.0) * level_of(splits[5], (D,), ((0, 8),), -0.4, 0.0), -2.0, 2.0)
    return dict(query_gate=query_gate, key_gate=key_gate, value_branch=value_branch, grad_out=grad_out, filters=filters, skip_bias=skip_bias)


def rounded_product(first, second):
    return lax.optimization_barrier((first.astype(jnp.float32) * second.astype(jnp.float32)).astype(jnp.bfloat16))


def reference(query_gate, key_gate, value_branch, grad_out, filters, skip_bias):
    gated = rounded_product(key_gate, value_branch)
    scaled = rounded_product(query_gate, grad_out)
    length, channels = gated.shape
    groups = filters.shape[0]
    per_group = channels // groups
    period = 2 * length
    gated_wide = gated.astype(jnp.float32)
    scaled_wide = scaled.astype(jnp.float32)
    gated_rows = gated_wide.T.reshape(groups, per_group, length)
    scaled_rows = scaled_wide.T.reshape(groups, per_group, length)

    def one_group(members):
        source, gradient, kernel = members
        source_wave = jnp.fft.rfft(source, n=period, axis=-1)
        gradient_wave = jnp.fft.rfft(gradient, n=period, axis=-1)
        kernel_wave = jnp.fft.rfft(kernel, n=period)
        forward = jnp.fft.irfft(source_wave * kernel_wave, n=period, axis=-1)[:, :length]
        backward = jnp.fft.irfft(gradient_wave * jnp.conj(kernel_wave), n=period, axis=-1)[:, :length]
        lagged = jnp.fft.irfft(gradient_wave * jnp.conj(source_wave), n=period, axis=-1)[:, :length]
        return forward, backward, jnp.sum(lagged, axis=0)

    forward, backward, grad_filters = lax.map(one_group, (gated_rows, scaled_rows, filters))
    forward = forward.reshape(channels, length).T
    backward = backward.reshape(channels, length).T
    convolved = lax.optimization_barrier((forward + skip_bias[None, :] * gated_wide).astype(jnp.bfloat16))
    correlated = lax.optimization_barrier((backward + skip_bias[None, :] * scaled_wide).astype(jnp.bfloat16))
    grad_query = (grad_out.astype(jnp.float32) * convolved.astype(jnp.float32)).astype(jnp.bfloat16)
    grad_key = (correlated.astype(jnp.float32) * value_branch.astype(jnp.float32)).astype(jnp.bfloat16)
    grad_value = (correlated.astype(jnp.float32) * key_gate.astype(jnp.float32)).astype(jnp.bfloat16)
    grad_bias = jnp.sum(scaled_wide * gated_wide, axis=0)
    return grad_query, grad_key, grad_value, grad_filters, grad_bias
```

```python
import jax
import jax.numpy as jnp
from jax import lax
from jax.experimental import pallas as pl
from jax.experimental.pallas import tpu as pltpu
from jax.sharding import PartitionSpec as P

CHANNELS = 16
EXTRA = 2 * CHANNELS
ROWS = EXTRA + 8
LANES = 128
WIDE = jnp.float32
NARROW = jnp.bfloat16


def gate_kernel(query_ref, key_ref, value_ref, grad_ref, filter_ref, out_ref):
    blocks = query_ref.shape[1] // LANES
    per_block = LANES // CHANNELS
    for block in range(blocks):
        columns = slice(block * LANES, (block + 1) * LANES)
        gated = (key_ref[:, columns].astype(WIDE) * value_ref[:, columns].astype(WIDE)).astype(NARROW)
        scaled = (query_ref[:, columns].astype(WIDE) * grad_ref[:, columns].astype(WIDE)).astype(NARROW)
        gated, scaled = gated.T, scaled.T
        for part in range(per_block):
            rows = slice(part * CHANNELS, (part + 1) * CHANNELS)
            out_ref[block * per_block + part, 0:CHANNELS, :] = gated[rows]
            out_ref[block * per_block + part, CHANNELS:EXTRA, :] = scaled[rows]
    for group in range(filter_ref.shape[0]):
        taps = jnp.broadcast_to(filter_ref[group : group + 1, :], (8, LANES))
        out_ref[group, EXTRA:ROWS, :] = taps.astype(NARROW)


def sequence_kernel(
    skip_ref, in_ref, out_ref, gated_ref, scaled_ref, taps_ref, rolled_ref, turned_ref, conv_ref, corr_ref, lag_ref
):
    count = in_ref.shape[0]
    pairs = count // 2
    height = pairs * CHANNELS
    for block in range(count):
        rows = slice(block // 2 * CHANNELS, (block // 2 + 1) * CHANNELS)
        columns = slice(block % 2 * LANES, (block % 2 + 1) * LANES)
        gated_ref[rows, columns] = in_ref[block, 0:CHANNELS, :]
        scaled_ref[rows, columns] = in_ref[block, CHANNELS:EXTRA, :]
        taps_ref[block : block + 1, :] = in_ref[block, EXTRA:ROWS, :].astype(WIDE)[0:1]
    scaled_ref[height:, :] = jnp.zeros((height, 2 * LANES), NARROW)

    row = lax.broadcasted_iota(jnp.int32, (LANES, LANES), 0)
    lane = lax.broadcasted_iota(jnp.int32, (LANES, LANES), 1)

    rolled_ref[0] = jnp.zeros((LANES, LANES), NARROW)
    before = jnp.zeros((LANES, LANES), WIDE)
    for block in range(count):
        now = jnp.broadcast_to(taps_ref[block : block + 1, :], (LANES, LANES))
        now = pltpu.roll(now, 0, 1, stride=1, stride_axis=0)
        rolled_ref[block + 1] = jnp.where(lane >= row, now, before).astype(NARROW)
        before = now

    flip = jnp.where(lane + row == LANES - 1, 1.0, 0.0).astype(NARROW)
    for half in range(2):
        turned_ref[half * LANES : (half + 1) * LANES, :] = lax.dot_general(
            flip,
            gated_ref[:, half * LANES : (half + 1) * LANES],
            (((1,), (1,)), ((), ())),
            preferred_element_type=WIDE,
        ).astype(NARROW)

    def finish(block, now, later):
        kept = jnp.where(lane <= row, now, later)
        lag_ref[block : block + 1, :] = jnp.sum(kept, axis=0, keepdims=True)

    pending = None
    odd = None
    for step in range(pairs):
        weights = jnp.concatenate(
            [
                jnp.concatenate([rolled_ref[2 * step + 1], rolled_ref[2 * step + 2]], axis=1),
                jnp.concatenate([rolled_ref[2 * step], rolled_ref[2 * step + 1]], axis=1),
            ],
            axis=0,
        )
        offset = step * CHANNELS
        conv = jnp.dot(gated_ref[: height - offset, :], weights, preferred_element_type=WIDE)
        corr = lax.dot_general(
            scaled_ref[offset:height, :], weights, (((1,), (1,)), ((), ())), preferred_element_type=WIDE
        )
        if step == 0:
            conv_ref[...] = conv
            corr_ref[...] = corr
        else:
            conv_ref[offset:, :] += conv
            corr_ref[: height - offset, :] += corr
        depth = min(height, -(-(height - offset) // 256) * 256)
        product = jnp.dot(
            turned_ref[:, :depth], scaled_ref[offset : offset + depth, :], preferred_element_type=WIDE
        )
        even = product[:LANES, :LANES] + product[LANES:, LANES:]
        even = pltpu.roll(even, 1, 1, stride=1, stride_axis=0)
        if step > 0:
            odd = odd + product[LANES:, :LANES]
            odd = pltpu.roll(odd, 1, 1, stride=1, stride_axis=0)
            finish(2 * step - 2, pending, odd)
            finish(2 * step - 1, odd, even)
        pending = even
        odd = product[:LANES, LANES:]
    odd = pltpu.roll(odd, 1, 1, stride=1, stride_axis=0)
    finish(count - 2, pending, odd)
    finish(count - 1, odd, jnp.zeros_like(odd))

    index = lax.axis_index("ctx")
    per_row = LANES // CHANNELS
    skip = skip_ref[pl.ds(index // per_row, 1), :]
    skip = pltpu.roll(jnp.broadcast_to(skip, (LANES, LANES)), LANES - index % per_row * CHANNELS, 1)
    skip = skip.T[:CHANNELS]
    skip = jnp.concatenate([skip, skip], axis=1)

    bias = jnp.zeros((CHANNELS, 2 * LANES), WIDE)
    for pair in range(pairs):
        rows = slice(pair * CHANNELS, (pair + 1) * CHANNELS)
        gated = gated_ref[rows, :].astype(WIDE)
        scaled = scaled_ref[rows, :].astype(WIDE)
        bias = bias + gated * scaled
        conv = (conv_ref[rows, :] + skip * gated).astype(NARROW)
        corr = (corr_ref[rows, :] + skip * scaled).astype(NARROW)
        for half in range(2):
            columns = slice(half * LANES, (half + 1) * LANES)
            out_ref[2 * pair + half, 0:CHANNELS, :] = conv[:, columns]
            out_ref[2 * pair + half, CHANNELS:EXTRA, :] = corr[:, columns]
    bias = jnp.broadcast_to(jnp.sum(bias, axis=1, keepdims=True), (CHANNELS, LANES))
    bias = jnp.concatenate([bias] * per_row, axis=0).T[0:1]
    bias_high = bias.astype(NARROW).astype(WIDE)
    bias_low = bias - bias_high
    place = lax.broadcasted_iota(jnp.int32, (8, LANES), 0)
    tail = jnp.where(place == 2, bias_high, jnp.where(place == 3, bias_low, 0.0))
    for block in range(count):
        lag = lag_ref[block : block + 1, :]
        lag_high = lag.astype(NARROW).astype(WIDE)
        tile = jnp.where(place == 0, lag_high, jnp.where(place == 1, lag - lag_high, tail))
        out_ref[block, EXTRA:ROWS, :] = tile.astype(NARROW)


def finish_kernel(in_ref, key_ref, value_ref, grad_ref, query_out, key_out, value_out, filter_out, bias_out):
    per_block = LANES // CHANNELS
    lane = lax.broadcasted_iota(jnp.int32, (1, LANES), 1) // CHANNELS
    for block in range(in_ref.shape[0] // per_block):
        columns = slice(block * LANES, (block + 1) * LANES)
        members = range(block * per_block, (block + 1) * per_block)
        conv = jnp.concatenate([in_ref[member, 0:CHANNELS, :] for member in members], axis=0).T.astype(WIDE)
        corr = jnp.concatenate([in_ref[member, CHANNELS:EXTRA, :] for member in members], axis=0).T.astype(WIDE)
        query_out[:, columns] = (grad_ref[:, columns].astype(WIDE) * conv).astype(NARROW)
        key_out[:, columns] = (corr * value_ref[:, columns].astype(WIDE)).astype(NARROW)
        value_out[:, columns] = (corr * key_ref[:, columns].astype(WIDE)).astype(NARROW)
        total = jnp.zeros((1, LANES), WIDE)
        for member in members:
            tile = in_ref[member, EXTRA:ROWS, :].astype(WIDE)
            filter_out[member : member + 1, :] = tile[0:1] + tile[1:2]
            total = total + jnp.where(lane == member % per_block, tile[2:3] + tile[3:4], 0.0)
        bias_out[block : block + 1, :] = total


def on_device(query_gate, key_gate, value_branch, grad_out, filters, skip_bias):
    tokens, channels = query_gate.shape
    count = lax.axis_size("ctx")
    height = count // 2 * CHANNELS
    message = jax.ShapeDtypeStruct((count, ROWS, LANES), NARROW)
    sent = pl.pallas_call(gate_kernel, out_shape=message, name="gate")(
        query_gate, key_gate, value_branch, grad_out, filters
    )
    moved = lax.all_to_all(sent, "ctx", split_axis=0, concat_axis=0, tiled=True)
    results = pl.pallas_call(
        sequence_kernel,
        out_shape=message,
        scratch_shapes=[
            pltpu.VMEM((height, 2 * LANES), NARROW),
            pltpu.VMEM((2 * height, 2 * LANES), NARROW),
            pltpu.VMEM((count, LANES), WIDE),
            pltpu.VMEM((count + 1, LANES, LANES), NARROW),
            pltpu.VMEM((2 * LANES, height), NARROW),
            pltpu.VMEM((height, 2 * LANES), WIDE),
            pltpu.VMEM((height, 2 * LANES), WIDE),
            pltpu.VMEM((count, LANES), WIDE),
        ],
        compiler_params=pltpu.CompilerParams(vmem_limit_bytes=48 * 1024 * 1024),
        name="sequence",
    )(skip_bias.reshape(channels // LANES, LANES), moved)
    back = lax.all_to_all(results, "ctx", split_axis=0, concat_axis=0, tiled=True)
    wide_out = jax.ShapeDtypeStruct((tokens, channels), NARROW)
    grad_query, grad_key, grad_value, grad_filters, grad_bias = pl.pallas_call(
        finish_kernel,
        out_shape=(
            wide_out,
            wide_out,
            wide_out,
            jax.ShapeDtypeStruct(filters.shape, WIDE),
            jax.ShapeDtypeStruct((channels // LANES, LANES), WIDE),
        ),
        name="finish",
    )(back, key_gate, value_branch, grad_out)
    return grad_query, grad_key, grad_value, grad_filters, grad_bias.reshape(channels)


def solution(mesh):
    in_specs = (
        P("ctx", "ch"),
        P("ctx", "ch"),
        P("ctx", "ch"),
        P("ctx", "ch"),
        P("ch", "ctx"),
        P("ch"),
    )
    out_specs = (P("ctx", "ch"), P("ctx", "ch"), P("ctx", "ch"), P("ch", "ctx"), P("ch"))
    return jax.shard_map(
        on_device, mesh=mesh, in_specs=in_specs, out_specs=out_specs, check_vma=False
    )
```

```python
import jax
import jax.numpy as jnp
from jax import lax
from jax.experimental import pallas as pl
from jax.experimental.pallas import tpu as pltpu
from jax.sharding import PartitionSpec as P

CHANNELS = 16
EXTRA = 2 * CHANNELS
ROWS = EXTRA + 2
LANES = 128
PIECE = 2 * LANES
WIDE = jnp.float32
NARROW = jnp.bfloat16


def gate_kernel(
    query_ref, key_ref, value_ref, grad_ref, filter_ref, out_ref, held_ref, taps_ref, sems, taps_sem
):
    per_block = LANES // CHANNELS
    pieces = query_ref.shape[1] // PIECE
    copies = []
    for piece in range(pieces):
        columns = pl.ds(piece * PIECE, PIECE)
        copies.append(
            [
                pltpu.make_async_copy(
                    source.at[:, columns], held_ref.at[place, :, columns], sems.at[piece, place]
                )
                for place, source in enumerate((key_ref, value_ref, query_ref, grad_ref))
            ]
        )
    taps_copy = pltpu.make_async_copy(filter_ref, taps_ref, taps_sem)
    for group in copies:
        for copy in group:
            copy.start()
    taps_copy.start()

    for piece in range(pieces):
        for copy in copies[piece]:
            copy.wait()
        for block in range(piece * PIECE // LANES, (piece + 1) * PIECE // LANES):
            columns = slice(block * LANES, (block + 1) * LANES)
            key, value, query, grad = (held_ref[place, :, columns].astype(WIDE) for place in range(4))
            gated = (key * value).astype(NARROW).T
            scaled = (query * grad).astype(NARROW).T
            for part in range(per_block):
                rows = slice(part * CHANNELS, (part + 1) * CHANNELS)
                first = (block * per_block + part) * ROWS
                out_ref[first : first + CHANNELS, :] = gated[rows]
                out_ref[first + CHANNELS : first + EXTRA, :] = scaled[rows]
    taps_copy.wait()
    for group in range(filter_ref.shape[0]):
        taps = jnp.broadcast_to(taps_ref[group : group + 1, :], (2, LANES))
        out_ref[group * ROWS + EXTRA : (group + 1) * ROWS, :] = taps.astype(NARROW)


def sequence_kernel(
    skip_ref, in_ref, out_ref, gated_ref, scaled_ref, taps_ref, rolled_ref, turned_ref, conv_ref, corr_ref, lag_ref
):
    count = in_ref.shape[0] // ROWS
    pairs = count // 2
    height = pairs * CHANNELS
    for block in range(count):
        rows = slice(block // 2 * CHANNELS, (block // 2 + 1) * CHANNELS)
        columns = slice(block % 2 * LANES, (block % 2 + 1) * LANES)
        first = block * ROWS
        gated_ref[rows, columns] = in_ref[first : first + CHANNELS, :]
        scaled_ref[rows, columns] = in_ref[first + CHANNELS : first + EXTRA, :]
        taps_ref[block : block + 1, :] = in_ref[first + EXTRA : first + ROWS, :].astype(WIDE)[0:1]
    scaled_ref[height:, :] = jnp.zeros((height, 2 * LANES), NARROW)

    row = lax.broadcasted_iota(jnp.int32, (LANES, LANES), 0)
    lane = lax.broadcasted_iota(jnp.int32, (LANES, LANES), 1)

    rolled_ref[0] = jnp.zeros((LANES, LANES), NARROW)
    before = jnp.zeros((LANES, LANES), WIDE)
    for block in range(count):
        now = jnp.broadcast_to(taps_ref[block : block + 1, :], (LANES, LANES))
        now = pltpu.roll(now, 0, 1, stride=1, stride_axis=0)
        rolled_ref[block + 1] = jnp.where(lane >= row, now, before).astype(NARROW)
        before = now

    flip = jnp.where(lane + row == LANES - 1, 1.0, 0.0).astype(NARROW)
    for half in range(2):
        turned_ref[half * LANES : (half + 1) * LANES, :] = lax.dot_general(
            flip,
            gated_ref[:, half * LANES : (half + 1) * LANES],
            (((1,), (1,)), ((), ())),
            preferred_element_type=WIDE,
        ).astype(NARROW)

    def finish(block, now, later):
        kept = jnp.where(lane <= row, now, later)
        lag_ref[block : block + 1, :] = jnp.sum(kept, axis=0, keepdims=True)

    pending = None
    odd = None
    for step in range(pairs):
        weights = jnp.concatenate(
            [
                jnp.concatenate([rolled_ref[2 * step + 1], rolled_ref[2 * step + 2]], axis=1),
                jnp.concatenate([rolled_ref[2 * step], rolled_ref[2 * step + 1]], axis=1),
            ],
            axis=0,
        )
        offset = step * CHANNELS
        conv = jnp.dot(gated_ref[: height - offset, :], weights, preferred_element_type=WIDE)
        corr = lax.dot_general(
            scaled_ref[offset:height, :], weights, (((1,), (1,)), ((), ())), preferred_element_type=WIDE
        )
        if step == 0:
            conv_ref[...] = conv
            corr_ref[...] = corr
        else:
            conv_ref[offset:, :] += conv
            corr_ref[: height - offset, :] += corr
        depth = min(height, -(-(height - offset) // 256) * 256)
        product = jnp.dot(
            turned_ref[:, :depth], scaled_ref[offset : offset + depth, :], preferred_element_type=WIDE
        )
        even = product[:LANES, :LANES] + product[LANES:, LANES:]
        even = pltpu.roll(even, 1, 1, stride=1, stride_axis=0)
        if step > 0:
            odd = odd + product[LANES:, :LANES]
            odd = pltpu.roll(odd, 1, 1, stride=1, stride_axis=0)
            finish(2 * step - 2, pending, odd)
            finish(2 * step - 1, odd, even)
        pending = even
        odd = product[:LANES, LANES:]
    odd = pltpu.roll(odd, 1, 1, stride=1, stride_axis=0)
    finish(count - 2, pending, odd)
    finish(count - 1, odd, jnp.zeros_like(odd))

    index = lax.axis_index("ctx")
    per_row = LANES // CHANNELS
    skip = skip_ref[pl.ds(index // per_row, 1), :]
    skip = pltpu.roll(jnp.broadcast_to(skip, (LANES, LANES)), LANES - index % per_row * CHANNELS, 1)
    skip = skip.T[:CHANNELS]
    skip = jnp.concatenate([skip, skip], axis=1)

    bias = jnp.zeros((CHANNELS, 2 * LANES), WIDE)
    for pair in range(pairs):
        rows = slice(pair * CHANNELS, (pair + 1) * CHANNELS)
        gated = gated_ref[rows, :].astype(WIDE)
        scaled = scaled_ref[rows, :].astype(WIDE)
        bias = bias + gated * scaled
        conv = (conv_ref[rows, :] + skip * gated).astype(NARROW)
        corr = (corr_ref[rows, :] + skip * scaled).astype(NARROW)
        for half in range(2):
            columns = slice(half * LANES, (half + 1) * LANES)
            first = (2 * pair + half) * ROWS
            out_ref[first : first + CHANNELS, :] = conv[:, columns]
            out_ref[first + CHANNELS : first + EXTRA, :] = corr[:, columns]
    bias = jnp.broadcast_to(jnp.sum(bias, axis=1, keepdims=True), (CHANNELS, LANES))
    bias = jnp.concatenate([bias] * per_row, axis=0).T[0:1]
    bias_high = bias.astype(NARROW).astype(WIDE)
    even = lax.broadcasted_iota(jnp.int32, (1, LANES), 1) // CHANNELS % 2 == 0
    tail = jnp.where(even, bias_high, bias - bias_high)
    for block in range(count):
        rows = jnp.concatenate([lag_ref[block : block + 1, :], tail], axis=0)
        out_ref[block * ROWS + EXTRA : (block + 1) * ROWS, :] = rows.astype(NARROW)


def finish_kernel(
    in_ref, key_ref, value_ref, grad_ref, query_out, key_out, value_out, filter_out, bias_out, held_ref, sems
):
    per_block = LANES // CHANNELS
    lane = lax.broadcasted_iota(jnp.int32, (1, LANES), 1) // CHANNELS
    copies = []
    for piece in range(key_ref.shape[1] // PIECE):
        for block in range(piece * PIECE // LANES, (piece + 1) * PIECE // LANES):
            columns = slice(block * LANES, (block + 1) * LANES)
            members = range(block * per_block, (block + 1) * per_block)

            def gather(offset):
                parts = [in_ref[member * ROWS + offset : member * ROWS + offset + CHANNELS, :] for member in members]
                return jnp.concatenate(parts, axis=0).T.astype(WIDE)

            conv, corr = gather(0), gather(CHANNELS)
            held_ref[0, :, columns] = (grad_ref[:, columns].astype(WIDE) * conv).astype(NARROW)
            held_ref[1, :, columns] = (corr * value_ref[:, columns].astype(WIDE)).astype(NARROW)
            held_ref[2, :, columns] = (corr * key_ref[:, columns].astype(WIDE)).astype(NARROW)
        columns = pl.ds(piece * PIECE, PIECE)
        for place, target in enumerate((query_out, key_out, value_out)):
            copy = pltpu.make_async_copy(
                held_ref.at[place, :, columns], target.at[:, columns], sems.at[piece, place]
            )
            copy.start()
            copies.append(copy)

    for block in range(key_ref.shape[1] // LANES):
        total = jnp.zeros((1, LANES), WIDE)
        for part in range(per_block):
            member = block * per_block + part
            rows = in_ref[member * ROWS + EXTRA : (member + 1) * ROWS, :].astype(WIDE)
            filter_out[member : member + 1, :] = rows[0:1]
            both = rows[1:2] + pltpu.roll(rows[1:2], CHANNELS, 1)
            total = total + jnp.where(lane == part, both, 0.0)
        bias_out[block : block + 1, :] = total
    for copy in copies:
        copy.wait()


def exchange(messages):
    count = lax.axis_size("ctx")
    split = messages.reshape(count, ROWS // 2, 2, LANES)
    return lax.all_to_all(split, "ctx", split_axis=0, concat_axis=0, tiled=True).reshape(messages.shape)


def on_device(query_gate, key_gate, value_branch, grad_out, filters, skip_bias):
    tokens, channels = query_gate.shape
    count = lax.axis_size("ctx")
    height = count // 2 * CHANNELS
    message = jax.ShapeDtypeStruct((count * ROWS, LANES), NARROW)
    grant = pltpu.CompilerParams(vmem_limit_bytes=16 * 1024 * 1024)
    hbm = pl.BlockSpec(memory_space=pltpu.HBM)
    vmem = pl.BlockSpec(memory_space=pltpu.VMEM)
    pieces = channels // PIECE
    sent = pl.pallas_call(
        gate_kernel,
        out_shape=message,
        in_specs=[hbm] * 5,
        out_specs=vmem,
        scratch_shapes=[
            pltpu.VMEM((4, tokens, channels), NARROW),
            pltpu.VMEM(filters.shape, WIDE),
            pltpu.SemaphoreType.DMA((pieces, 4)),
            pltpu.SemaphoreType.DMA,
        ],
        compiler_params=grant,
        name="gate",
    )(
        *(
            pltpu.with_memory_space_constraint(argument, pltpu.HBM)
            for argument in (query_gate, key_gate, value_branch, grad_out, filters)
        )
    )
    moved = exchange(sent)
    results = pl.pallas_call(
        sequence_kernel,
        out_shape=message,
        scratch_shapes=[
            pltpu.VMEM((height, 2 * LANES), NARROW),
            pltpu.VMEM((2 * height, 2 * LANES), NARROW),
            pltpu.VMEM((count, LANES), WIDE),
            pltpu.VMEM((count + 1, LANES, LANES), NARROW),
            pltpu.VMEM((2 * LANES, height), NARROW),
            pltpu.VMEM((height, 2 * LANES), WIDE),
            pltpu.VMEM((height, 2 * LANES), WIDE),
            pltpu.VMEM((count, LANES), WIDE),
        ],
        compiler_params=grant,
        name="sequence",
    )(skip_bias.reshape(channels // LANES, LANES), moved)
    back = exchange(results)
    wide_out = jax.ShapeDtypeStruct((tokens, channels), NARROW)
    grad_query, grad_key, grad_value, grad_filters, grad_bias = pl.pallas_call(
        finish_kernel,
        out_shape=(
            wide_out,
            wide_out,
            wide_out,
            jax.ShapeDtypeStruct(filters.shape, WIDE),
            jax.ShapeDtypeStruct((channels // LANES, LANES), WIDE),
        ),
        in_specs=[vmem] * 4,
        out_specs=(hbm, hbm, hbm, vmem, vmem),
        scratch_shapes=[
            pltpu.VMEM((3, tokens, channels), NARROW),
            pltpu.SemaphoreType.DMA((pieces, 3)),
        ],
        compiler_params=grant,
        name="finish",
    )(back, key_gate, value_branch, grad_out)
    return grad_query, grad_key, grad_value, grad_filters, grad_bias.reshape(channels)


def solution(mesh):
    in_specs = (
        P("ctx", "ch"),
        P("ctx", "ch"),
        P("ctx", "ch"),
        P("ctx", "ch"),
        P("ch", "ctx"),
        P("ch"),
    )
    out_specs = (P("ctx", "ch"), P("ctx", "ch"), P("ctx", "ch"), P("ch", "ctx"), P("ch"))
    return jax.shard_map(
        on_device, mesh=mesh, in_specs=in_specs, out_specs=out_specs, check_vma=False
    )
```

```python
import jax
import jax.numpy as jnp
from jax import lax
from jax.experimental import pallas as pl
from jax.experimental.pallas import tpu as pltpu
from jax.sharding import PartitionSpec as P

CHANNELS = 16
EXTRA = 2 * CHANNELS
ROWS = EXTRA + 2
LANES = 128
PIECE = 2 * LANES
SIDE = 4
STEP = 9
WIDE = jnp.float32
NARROW = jnp.bfloat16


def listing(count):
    ring = count // SIDE
    return [STEP * turn % ring * SIDE + place for place in range(SIDE) for turn in range(ring)]


def first_rows(count):
    order = listing(count)
    return [order.index(device) * ROWS for device in range(count)]


def gate_kernel(
    query_ref, key_ref, value_ref, grad_ref, filter_ref, out_ref, held_ref, taps_ref, sems, taps_sem
):
    per_block = LANES // CHANNELS
    pieces = query_ref.shape[1] // PIECE
    starts = first_rows(filter_ref.shape[0])
    copies = []
    for piece in range(pieces):
        columns = pl.ds(piece * PIECE, PIECE)
        copies.append(
            [
                pltpu.make_async_copy(
                    source.at[:, columns], held_ref.at[place, :, columns], sems.at[piece, place]
                )
                for place, source in enumerate((key_ref, value_ref, query_ref, grad_ref))
            ]
        )
    taps_copy = pltpu.make_async_copy(filter_ref, taps_ref, taps_sem)
    for group in copies:
        for copy in group:
            copy.start()
    taps_copy.start()

    for piece in range(pieces):
        for copy in copies[piece]:
            copy.wait()
        for block in range(piece * PIECE // LANES, (piece + 1) * PIECE // LANES):
            columns = slice(block * LANES, (block + 1) * LANES)
            key, value, query, grad = (held_ref[place, :, columns].astype(WIDE) for place in range(4))
            gated = (key * value).astype(NARROW).T
            scaled = (query * grad).astype(NARROW).T
            for part in range(per_block):
                rows = slice(part * CHANNELS, (part + 1) * CHANNELS)
                first = starts[block * per_block + part]
                out_ref[first : first + CHANNELS, :] = gated[rows]
                out_ref[first + CHANNELS : first + EXTRA, :] = scaled[rows]
    taps_copy.wait()
    for group in range(filter_ref.shape[0]):
        taps = jnp.broadcast_to(taps_ref[group : group + 1, :], (2, LANES))
        out_ref[starts[group] + EXTRA : starts[group] + ROWS, :] = taps.astype(NARROW)


def sequence_kernel(
    skip_ref, in_ref, out_ref, gated_ref, scaled_ref, taps_ref, rolled_ref, turned_ref, conv_ref, corr_ref, lag_ref
):
    count = in_ref.shape[0] // ROWS
    starts = first_rows(count)
    pairs = count // 2
    height = pairs * CHANNELS
    for block in range(count):
        rows = slice(block // 2 * CHANNELS, (block // 2 + 1) * CHANNELS)
        columns = slice(block % 2 * LANES, (block % 2 + 1) * LANES)
        first = starts[block]
        gated_ref[rows, columns] = in_ref[first : first + CHANNELS, :]
        scaled_ref[rows, columns] = in_ref[first + CHANNELS : first + EXTRA, :]
        taps_ref[block : block + 1, :] = in_ref[first + EXTRA : first + ROWS, :].astype(WIDE)[0:1]
    scaled_ref[height:, :] = jnp.zeros((height, 2 * LANES), NARROW)

    row = lax.broadcasted_iota(jnp.int32, (LANES, LANES), 0)
    lane = lax.broadcasted_iota(jnp.int32, (LANES, LANES), 1)

    rolled_ref[0] = jnp.zeros((LANES, LANES), NARROW)
    before = jnp.zeros((LANES, LANES), WIDE)
    for block in range(count):
        now = jnp.broadcast_to(taps_ref[block : block + 1, :], (LANES, LANES))
        now = pltpu.roll(now, 0, 1, stride=1, stride_axis=0)
        rolled_ref[block + 1] = jnp.where(lane >= row, now, before).astype(NARROW)
        before = now

    flip = jnp.where(lane + row == LANES - 1, 1.0, 0.0).astype(NARROW)
    for half in range(2):
        turned_ref[half * LANES : (half + 1) * LANES, :] = lax.dot_general(
            flip,
            gated_ref[:, half * LANES : (half + 1) * LANES],
            (((1,), (1,)), ((), ())),
            preferred_element_type=WIDE,
        ).astype(NARROW)

    def finish(block, now, later):
        kept = jnp.where(lane <= row, now, later)
        lag_ref[block : block + 1, :] = jnp.sum(kept, axis=0, keepdims=True)

    pending = None
    odd = None
    for step in range(pairs):
        weights = jnp.concatenate(
            [
                jnp.concatenate([rolled_ref[2 * step + 1], rolled_ref[2 * step + 2]], axis=1),
                jnp.concatenate([rolled_ref[2 * step], rolled_ref[2 * step + 1]], axis=1),
            ],
            axis=0,
        )
        offset = step * CHANNELS
        conv = jnp.dot(gated_ref[: height - offset, :], weights, preferred_element_type=WIDE)
        corr = lax.dot_general(
            scaled_ref[offset:height, :], weights, (((1,), (1,)), ((), ())), preferred_element_type=WIDE
        )
        if step == 0:
            conv_ref[...] = conv
            corr_ref[...] = corr
        else:
            conv_ref[offset:, :] += conv
            corr_ref[: height - offset, :] += corr
        depth = min(height, -(-(height - offset) // 256) * 256)
        product = jnp.dot(
            turned_ref[:, :depth], scaled_ref[offset : offset + depth, :], preferred_element_type=WIDE
        )
        even = product[:LANES, :LANES] + product[LANES:, LANES:]
        even = pltpu.roll(even, 1, 1, stride=1, stride_axis=0)
        if step > 0:
            odd = odd + product[LANES:, :LANES]
            odd = pltpu.roll(odd, 1, 1, stride=1, stride_axis=0)
            finish(2 * step - 2, pending, odd)
            finish(2 * step - 1, odd, even)
        pending = even
        odd = product[:LANES, LANES:]
    odd = pltpu.roll(odd, 1, 1, stride=1, stride_axis=0)
    finish(count - 2, pending, odd)
    finish(count - 1, odd, jnp.zeros_like(odd))

    index = lax.axis_index("ctx")
    per_row = LANES // CHANNELS
    skip = skip_ref[pl.ds(index // per_row, 1), :]
    skip = pltpu.roll(jnp.broadcast_to(skip, (LANES, LANES)), LANES - index % per_row * CHANNELS, 1)
    skip = skip.T[:CHANNELS]
    skip = jnp.concatenate([skip, skip], axis=1)

    bias = jnp.zeros((CHANNELS, 2 * LANES), WIDE)
    for pair in range(pairs):
        rows = slice(pair * CHANNELS, (pair + 1) * CHANNELS)
        gated = gated_ref[rows, :].astype(WIDE)
        scaled = scaled_ref[rows, :].astype(WIDE)
        bias = bias + gated * scaled
        conv = (conv_ref[rows, :] + skip * gated).astype(NARROW)
        corr = (corr_ref[rows, :] + skip * scaled).astype(NARROW)
        for half in range(2):
            columns = slice(half * LANES, (half + 1) * LANES)
            first = starts[2 * pair + half]
            out_ref[first : first + CHANNELS, :] = conv[:, columns]
            out_ref[first + CHANNELS : first + EXTRA, :] = corr[:, columns]
    bias = jnp.broadcast_to(jnp.sum(bias, axis=1, keepdims=True), (CHANNELS, LANES))
    bias = jnp.concatenate([bias] * per_row, axis=0).T[0:1]
    bias_high = bias.astype(NARROW).astype(WIDE)
    even = lax.broadcasted_iota(jnp.int32, (1, LANES), 1) // CHANNELS % 2 == 0
    tail = jnp.where(even, bias_high, bias - bias_high)
    for block in range(count):
        rows = jnp.concatenate([lag_ref[block : block + 1, :], tail], axis=0)
        out_ref[starts[block] + EXTRA : starts[block] + ROWS, :] = rows.astype(NARROW)


def finish_kernel(
    in_ref, key_ref, value_ref, grad_ref, query_out, key_out, value_out, filter_out, bias_out, held_ref, sems
):
    per_block = LANES // CHANNELS
    lane = lax.broadcasted_iota(jnp.int32, (1, LANES), 1) // CHANNELS
    starts = first_rows(filter_out.shape[0])
    copies = []
    for piece in range(key_ref.shape[1] // PIECE):
        for block in range(piece * PIECE // LANES, (piece + 1) * PIECE // LANES):
            columns = slice(block * LANES, (block + 1) * LANES)
            members = range(block * per_block, (block + 1) * per_block)

            def gather(offset):
                parts = [in_ref[starts[member] + offset : starts[member] + offset + CHANNELS, :] for member in members]
                return jnp.concatenate(parts, axis=0).T.astype(WIDE)

            conv, corr = gather(0), gather(CHANNELS)
            held_ref[0, :, columns] = (grad_ref[:, columns].astype(WIDE) * conv).astype(NARROW)
            held_ref[1, :, columns] = (corr * value_ref[:, columns].astype(WIDE)).astype(NARROW)
            held_ref[2, :, columns] = (corr * key_ref[:, columns].astype(WIDE)).astype(NARROW)
        columns = pl.ds(piece * PIECE, PIECE)
        for place, target in enumerate((query_out, key_out, value_out)):
            copy = pltpu.make_async_copy(
                held_ref.at[place, :, columns], target.at[:, columns], sems.at[piece, place]
            )
            copy.start()
            copies.append(copy)

    for block in range(key_ref.shape[1] // LANES):
        total = jnp.zeros((1, LANES), WIDE)
        for part in range(per_block):
            member = block * per_block + part
            rows = in_ref[starts[member] + EXTRA : starts[member] + ROWS, :].astype(WIDE)
            filter_out[member : member + 1, :] = rows[0:1]
            both = rows[1:2] + pltpu.roll(rows[1:2], CHANNELS, 1)
            total = total + jnp.where(lane == part, both, 0.0)
        bias_out[block : block + 1, :] = total
    for copy in copies:
        copy.wait()


def exchange(messages):
    count = lax.axis_size("ctx")
    split = messages.reshape(count, ROWS // 2, 2, LANES)
    moved = lax.all_to_all(
        split, "ctx", split_axis=0, concat_axis=0, tiled=True, axis_index_groups=[listing(count)]
    )
    return moved.reshape(messages.shape)


def on_device(query_gate, key_gate, value_branch, grad_out, filters, skip_bias):
    tokens, channels = query_gate.shape
    count = lax.axis_size("ctx")
    height = count // 2 * CHANNELS
    message = jax.ShapeDtypeStruct((count * ROWS, LANES), NARROW)
    grant = pltpu.CompilerParams(vmem_limit_bytes=16 * 1024 * 1024)
    hbm = pl.BlockSpec(memory_space=pltpu.HBM)
    vmem = pl.BlockSpec(memory_space=pltpu.VMEM)
    pieces = channels // PIECE
    sent = pl.pallas_call(
        gate_kernel,
        out_shape=message,
        in_specs=[hbm] * 5,
        out_specs=vmem,
        scratch_shapes=[
            pltpu.VMEM((4, tokens, channels), NARROW),
            pltpu.VMEM(filters.shape, WIDE),
            pltpu.SemaphoreType.DMA((pieces, 4)),
            pltpu.SemaphoreType.DMA,
        ],
        compiler_params=grant,
        name="gate",
    )(
        *(
            pltpu.with_memory_space_constraint(argument, pltpu.HBM)
            for argument in (query_gate, key_gate, value_branch, grad_out, filters)
        )
    )
    moved = exchange(sent)
    results = pl.pallas_call(
        sequence_kernel,
        out_shape=message,
        scratch_shapes=[
            pltpu.VMEM((height, 2 * LANES), NARROW),
            pltpu.VMEM((2 * height, 2 * LANES), NARROW),
            pltpu.VMEM((count, LANES), WIDE),
            pltpu.VMEM((count + 1, LANES, LANES), NARROW),
            pltpu.VMEM((2 * LANES, height), NARROW),
            pltpu.VMEM((height, 2 * LANES), WIDE),
            pltpu.VMEM((height, 2 * LANES), WIDE),
            pltpu.VMEM((count, LANES), WIDE),
        ],
        compiler_params=grant,
        name="sequence",
    )(skip_bias.reshape(channels // LANES, LANES), moved)
    back = exchange(results)
    wide_out = jax.ShapeDtypeStruct((tokens, channels), NARROW)
    grad_query, grad_key, grad_value, grad_filters, grad_bias = pl.pallas_call(
        finish_kernel,
        out_shape=(
            wide_out,
            wide_out,
            wide_out,
            jax.ShapeDtypeStruct(filters.shape, WIDE),
            jax.ShapeDtypeStruct((channels // LANES, LANES), WIDE),
        ),
        in_specs=[vmem] * 4,
        out_specs=(hbm, hbm, hbm, vmem, vmem),
        scratch_shapes=[
            pltpu.VMEM((3, tokens, channels), NARROW),
            pltpu.SemaphoreType.DMA((pieces, 3)),
        ],
        compiler_params=grant,
        name="finish",
    )(back, key_gate, value_branch, grad_out)
    return grad_query, grad_key, grad_value, grad_filters, grad_bias.reshape(channels)


def solution(mesh):
    in_specs = (
        P("ctx", "ch"),
        P("ctx", "ch"),
        P("ctx", "ch"),
        P("ctx", "ch"),
        P("ch", "ctx"),
        P("ch"),
    )
    out_specs = (P("ctx", "ch"), P("ctx", "ch"), P("ctx", "ch"), P("ch", "ctx"), P("ch"))
    return jax.shard_map(
        on_device, mesh=mesh, in_specs=in_specs, out_specs=out_specs, check_vma=False
    )
```

```python
import jax
import jax.numpy as jnp
from jax import lax
from jax.experimental import pallas as pl
from jax.experimental.pallas import tpu as pltpu
from jax.sharding import PartitionSpec as P

CHANNELS = 16
EXTRA = 2 * CHANNELS
ROWS = EXTRA + 2
LANES = 128
PIECE = 4 * LANES
SIDE = 4
STEP = 9
WIDE = jnp.float32
NARROW = jnp.bfloat16


def listing(count):
    ring = count // SIDE
    return [STEP * turn % ring * SIDE + place for place in range(SIDE) for turn in range(ring)]


def first_rows(count):
    order = listing(count)
    return [order.index(device) * ROWS for device in range(count)]


def gate_kernel(
    query_ref, key_ref, value_ref, grad_ref, filter_ref, out_ref, held_ref, taps_ref, sems, taps_sem
):
    per_block = LANES // CHANNELS
    pieces = query_ref.shape[1] // PIECE
    starts = first_rows(filter_ref.shape[0])
    copies = []
    for piece in range(pieces):
        columns = pl.ds(piece * PIECE, PIECE)
        copies.append(
            [
                pltpu.make_async_copy(
                    source.at[:, columns], held_ref.at[place, :, columns], sems.at[piece, place]
                )
                for place, source in enumerate((key_ref, value_ref, query_ref, grad_ref))
            ]
        )
    taps_copy = pltpu.make_async_copy(filter_ref, taps_ref, taps_sem)
    for group in copies:
        for copy in group:
            copy.start()
    taps_copy.start()

    for piece in range(pieces):
        for copy in copies[piece]:
            copy.wait()
        for block in range(piece * PIECE // LANES, (piece + 1) * PIECE // LANES):
            columns = slice(block * LANES, (block + 1) * LANES)
            key, value, query, grad = (held_ref[place, :, columns] for place in range(4))
            both = jnp.concatenate([key * value, query * grad], axis=1).T
            gated, scaled = both[:LANES], both[LANES:]
            for part in range(per_block):
                rows = slice(part * CHANNELS, (part + 1) * CHANNELS)
                first = starts[block * per_block + part]
                out_ref[first : first + CHANNELS, :] = gated[rows]
                out_ref[first + CHANNELS : first + EXTRA, :] = scaled[rows]
    taps_copy.wait()
    for group in range(filter_ref.shape[0]):
        taps = jnp.broadcast_to(taps_ref[group : group + 1, :], (2, LANES))
        out_ref[starts[group] + EXTRA : starts[group] + ROWS, :] = taps.astype(NARROW)


def sequence_kernel(
    skip_ref, in_ref, out_ref, gated_ref, scaled_ref, taps_ref, rolled_ref, turned_ref, conv_ref, corr_ref, lag_ref
):
    count = in_ref.shape[0] // ROWS
    starts = first_rows(count)
    pairs = count // 2
    height = pairs * CHANNELS
    for block in range(count):
        rows = slice(block // 2 * CHANNELS, (block // 2 + 1) * CHANNELS)
        columns = slice(block % 2 * LANES, (block % 2 + 1) * LANES)
        first = starts[block]
        gated_ref[rows, columns] = in_ref[first : first + CHANNELS, :]
        scaled_ref[rows, columns] = in_ref[first + CHANNELS : first + EXTRA, :]
        taps_ref[block : block + 1, :] = in_ref[first + EXTRA : first + ROWS, :].astype(WIDE)[0:1]
    scaled_ref[height:, :] = jnp.zeros((height, 2 * LANES), NARROW)

    row = lax.broadcasted_iota(jnp.int32, (LANES, LANES), 0)
    lane = lax.broadcasted_iota(jnp.int32, (LANES, LANES), 1)

    rolled_ref[0] = jnp.zeros((LANES, LANES), NARROW)
    before = jnp.zeros((LANES, LANES), WIDE)
    for block in range(count):
        now = jnp.broadcast_to(taps_ref[block : block + 1, :], (LANES, LANES))
        now = pltpu.roll(now, 0, 1, stride=1, stride_axis=0)
        rolled_ref[block + 1] = jnp.where(lane >= row, now, before).astype(NARROW)
        before = now

    flip = jnp.where(lane + row == LANES - 1, 1.0, 0.0).astype(NARROW)
    for half in range(2):
        turned_ref[half * LANES : (half + 1) * LANES, :] = lax.dot_general(
            flip,
            gated_ref[:, half * LANES : (half + 1) * LANES],
            (((1,), (1,)), ((), ())),
            preferred_element_type=WIDE,
        ).astype(NARROW)

    def finish(block, now, later):
        kept = jnp.where(lane <= row, now, later)
        lag_ref[block : block + 1, :] = jnp.sum(kept, axis=0, keepdims=True)

    pending = None
    odd = None
    for step in range(pairs):
        weights = jnp.concatenate(
            [
                jnp.concatenate([rolled_ref[2 * step + 1], rolled_ref[2 * step + 2]], axis=1),
                jnp.concatenate([rolled_ref[2 * step], rolled_ref[2 * step + 1]], axis=1),
            ],
            axis=0,
        )
        offset = step * CHANNELS
        conv = jnp.dot(gated_ref[: height - offset, :], weights, preferred_element_type=WIDE)
        corr = lax.dot_general(
            scaled_ref[offset:height, :], weights, (((1,), (1,)), ((), ())), preferred_element_type=WIDE
        )
        if step == 0:
            conv_ref[...] = conv
            corr_ref[...] = corr
        else:
            conv_ref[offset:, :] += conv
            corr_ref[: height - offset, :] += corr
        depth = min(height, -(-(height - offset) // 256) * 256)
        product = jnp.dot(
            turned_ref[:, :depth], scaled_ref[offset : offset + depth, :], preferred_element_type=WIDE
        )
        even = product[:LANES, :LANES] + product[LANES:, LANES:]
        even = pltpu.roll(even, 1, 1, stride=1, stride_axis=0)
        if step > 0:
            odd = odd + product[LANES:, :LANES]
            odd = pltpu.roll(odd, 1, 1, stride=1, stride_axis=0)
            finish(2 * step - 2, pending, odd)
            finish(2 * step - 1, odd, even)
        pending = even
        odd = product[:LANES, LANES:]
    odd = pltpu.roll(odd, 1, 1, stride=1, stride_axis=0)
    finish(count - 2, pending, odd)
    finish(count - 1, odd, jnp.zeros_like(odd))

    index = lax.axis_index("ctx")
    per_row = LANES // CHANNELS
    skip = skip_ref[pl.ds(index // per_row, 1), :]
    skip = pltpu.roll(jnp.broadcast_to(skip, (LANES, LANES)), LANES - index % per_row * CHANNELS, 1)
    skip = skip.T[:CHANNELS]
    skip = jnp.concatenate([skip, skip], axis=1)

    bias = jnp.zeros((CHANNELS, 2 * LANES), WIDE)
    for pair in range(pairs):
        rows = slice(pair * CHANNELS, (pair + 1) * CHANNELS)
        gated = gated_ref[rows, :].astype(WIDE)
        scaled = scaled_ref[rows, :].astype(WIDE)
        bias = bias + gated * scaled
        conv = (conv_ref[rows, :] + skip * gated).astype(NARROW)
        corr = (corr_ref[rows, :] + skip * scaled).astype(NARROW)
        for half in range(2):
            columns = slice(half * LANES, (half + 1) * LANES)
            first = starts[2 * pair + half]
            out_ref[first : first + CHANNELS, :] = conv[:, columns]
            out_ref[first + CHANNELS : first + EXTRA, :] = corr[:, columns]
    bias = jnp.broadcast_to(jnp.sum(bias, axis=1, keepdims=True), (CHANNELS, LANES))
    bias = jnp.concatenate([bias] * per_row, axis=0).T[0:1]
    bias_high = bias.astype(NARROW).astype(WIDE)
    even = lax.broadcasted_iota(jnp.int32, (1, LANES), 1) // CHANNELS % 2 == 0
    tail = jnp.where(even, bias_high, bias - bias_high)
    for block in range(count):
        rows = jnp.concatenate([lag_ref[block : block + 1, :], tail], axis=0)
        out_ref[starts[block] + EXTRA : starts[block] + ROWS, :] = rows.astype(NARROW)


def finish_kernel(
    in_ref, key_ref, value_ref, grad_ref, query_out, key_out, value_out, filter_out, bias_out, held_ref, sems
):
    per_block = LANES // CHANNELS
    lane = lax.broadcasted_iota(jnp.int32, (1, LANES), 1) // CHANNELS
    starts = first_rows(filter_out.shape[0])
    copies = []
    for piece in range(key_ref.shape[1] // PIECE):
        for block in range(piece * PIECE // LANES, (piece + 1) * PIECE // LANES):
            columns = slice(block * LANES, (block + 1) * LANES)
            members = range(block * per_block, (block + 1) * per_block)

            def gather(offset):
                parts = [in_ref[starts[member] + offset : starts[member] + offset + CHANNELS, :] for member in members]
                return jnp.concatenate(parts, axis=0).T

            conv, corr = gather(0), gather(CHANNELS)
            held_ref[0, :, columns] = grad_ref[:, columns] * conv
            held_ref[1, :, columns] = corr * value_ref[:, columns]
            held_ref[2, :, columns] = corr * key_ref[:, columns]
        columns = pl.ds(piece * PIECE, PIECE)
        for place, target in enumerate((query_out, key_out, value_out)):
            copy = pltpu.make_async_copy(
                held_ref.at[place, :, columns], target.at[:, columns], sems.at[piece, place]
            )
            copy.start()
            copies.append(copy)

    for block in range(key_ref.shape[1] // LANES):
        total = jnp.zeros((1, LANES), WIDE)
        for part in range(per_block):
            member = block * per_block + part
            rows = in_ref[starts[member] + EXTRA : starts[member] + ROWS, :].astype(WIDE)
            filter_out[member : member + 1, :] = rows[0:1]
            both = rows[1:2] + pltpu.roll(rows[1:2], CHANNELS, 1)
            total = total + jnp.where(lane == part, both, 0.0)
        bias_out[block : block + 1, :] = total
    for copy in copies:
        copy.wait()


def exchange(messages):
    count = lax.axis_size("ctx")
    split = messages.reshape(count, ROWS // 2, 2, LANES)
    moved = lax.all_to_all(
        split, "ctx", split_axis=0, concat_axis=0, tiled=True, axis_index_groups=[listing(count)]
    )
    return moved.reshape(messages.shape)


def on_device(query_gate, key_gate, value_branch, grad_out, filters, skip_bias):
    tokens, channels = query_gate.shape
    count = lax.axis_size("ctx")
    height = count // 2 * CHANNELS
    message = jax.ShapeDtypeStruct((count * ROWS, LANES), NARROW)
    grant = pltpu.CompilerParams(vmem_limit_bytes=16 * 1024 * 1024)
    hbm = pl.BlockSpec(memory_space=pltpu.HBM)
    vmem = pl.BlockSpec(memory_space=pltpu.VMEM)
    pieces = channels // PIECE
    sent = pl.pallas_call(
        gate_kernel,
        out_shape=message,
        in_specs=[hbm] * 5,
        out_specs=vmem,
        scratch_shapes=[
            pltpu.VMEM((4, tokens, channels), NARROW),
            pltpu.VMEM(filters.shape, WIDE),
            pltpu.SemaphoreType.DMA((pieces, 4)),
            pltpu.SemaphoreType.DMA,
        ],
        compiler_params=grant,
        name="gate",
    )(
        *(
            pltpu.with_memory_space_constraint(argument, pltpu.HBM)
            for argument in (query_gate, key_gate, value_branch, grad_out, filters)
        )
    )
    moved = exchange(sent)
    results = pl.pallas_call(
        sequence_kernel,
        out_shape=message,
        scratch_shapes=[
            pltpu.VMEM((height, 2 * LANES), NARROW),
            pltpu.VMEM((2 * height, 2 * LANES), NARROW),
            pltpu.VMEM((count, LANES), WIDE),
            pltpu.VMEM((count + 1, LANES, LANES), NARROW),
            pltpu.VMEM((2 * LANES, height), NARROW),
            pltpu.VMEM((height, 2 * LANES), WIDE),
            pltpu.VMEM((height, 2 * LANES), WIDE),
            pltpu.VMEM((count, LANES), WIDE),
        ],
        compiler_params=grant,
        name="sequence",
    )(skip_bias.reshape(channels // LANES, LANES), moved)
    back = exchange(results)
    wide_out = jax.ShapeDtypeStruct((tokens, channels), NARROW)
    grad_query, grad_key, grad_value, grad_filters, grad_bias = pl.pallas_call(
        finish_kernel,
        out_shape=(
            wide_out,
            wide_out,
            wide_out,
            jax.ShapeDtypeStruct(filters.shape, WIDE),
            jax.ShapeDtypeStruct((channels // LANES, LANES), WIDE),
        ),
        in_specs=[vmem] * 4,
        out_specs=(hbm, hbm, hbm, vmem, vmem),
        scratch_shapes=[
            pltpu.VMEM((3, tokens, channels), NARROW),
            pltpu.SemaphoreType.DMA((pieces, 3)),
        ],
        compiler_params=grant,
        name="finish",
    )(back, key_gate, value_branch, grad_out)
    return grad_query, grad_key, grad_value, grad_filters, grad_bias.reshape(channels)


def solution(mesh):
    in_specs = (
        P("ctx", "ch"),
        P("ctx", "ch"),
        P("ctx", "ch"),
        P("ctx", "ch"),
        P("ch", "ctx"),
        P("ch"),
    )
    out_specs = (P("ctx", "ch"), P("ctx", "ch"), P("ctx", "ch"), P("ch", "ctx"), P("ch"))
    return jax.shard_map(
        on_device, mesh=mesh, in_specs=in_specs, out_specs=out_specs, check_vma=False
    )
```

```python
import jax
import jax.numpy as jnp
from jax import lax
from jax.experimental import pallas as pl
from jax.experimental.pallas import tpu as pltpu
from jax.sharding import PartitionSpec as P

CHANNELS = 16
EXTRA = 2 * CHANNELS
ROWS = EXTRA + 2
LANES = 128
PIECE = 4 * LANES
SIDE = 4
STEP = 9
STEP_BACK = 13
WIDE = jnp.float32
NARROW = jnp.bfloat16


def listing(count, back=False):
    ring = count // SIDE
    step = STEP_BACK if back else STEP
    return [step * turn % ring * SIDE + place for place in range(SIDE) for turn in range(ring)]


def first_rows(count, back=False):
    order = listing(count, back)
    return [order.index(device) * ROWS for device in range(count)]


def gate_kernel(
    query_ref, key_ref, value_ref, grad_ref, filter_ref, out_ref, held_ref, taps_ref, sems, taps_sem
):
    per_block = LANES // CHANNELS
    pieces = query_ref.shape[1] // PIECE
    starts = first_rows(filter_ref.shape[0])
    copies = []
    for piece in range(pieces):
        columns = pl.ds(piece * PIECE, PIECE)
        copies.append(
            [
                pltpu.make_async_copy(
                    source.at[:, columns], held_ref.at[place, :, columns], sems.at[piece, place]
                )
                for place, source in enumerate((key_ref, value_ref, query_ref, grad_ref))
            ]
        )
    taps_copy = pltpu.make_async_copy(filter_ref, taps_ref, taps_sem)
    for group in copies:
        for copy in group:
            copy.start()
    taps_copy.start()

    for piece in range(pieces):
        for copy in copies[piece]:
            copy.wait()
        for block in range(piece * PIECE // LANES, (piece + 1) * PIECE // LANES):
            columns = slice(block * LANES, (block + 1) * LANES)
            key, value, query, grad = (held_ref[place, :, columns] for place in range(4))
            gated = (key * value).T
            scaled = (query * grad).T
            for part in range(per_block):
                rows = slice(part * CHANNELS, (part + 1) * CHANNELS)
                first = starts[block * per_block + part]
                out_ref[first : first + CHANNELS, :] = gated[rows]
                out_ref[first + CHANNELS : first + EXTRA, :] = scaled[rows]
    taps_copy.wait()
    for group in range(filter_ref.shape[0]):
        taps = jnp.broadcast_to(taps_ref[group : group + 1, :], (2, LANES))
        out_ref[starts[group] + EXTRA : starts[group] + ROWS, :] = taps.astype(NARROW)


def sequence_kernel(
    skip_ref, in_ref, out_ref, gated_ref, scaled_ref, taps_ref, rolled_ref, turned_ref, conv_ref, corr_ref, lag_ref
):
    count = in_ref.shape[0] // ROWS
    starts = first_rows(count)
    starts_back = first_rows(count, True)
    pairs = count // 2
    height = pairs * CHANNELS
    for block in range(count):
        rows = slice(block // 2 * CHANNELS, (block // 2 + 1) * CHANNELS)
        columns = slice(block % 2 * LANES, (block % 2 + 1) * LANES)
        first = starts[block]
        gated_ref[rows, columns] = in_ref[first : first + CHANNELS, :]
        scaled_ref[rows, columns] = in_ref[first + CHANNELS : first + EXTRA, :]
        taps_ref[block : block + 1, :] = in_ref[first + EXTRA : first + ROWS, :].astype(WIDE)[0:1]
    scaled_ref[height:, :] = jnp.zeros((height, 2 * LANES), NARROW)

    row = lax.broadcasted_iota(jnp.int32, (LANES, LANES), 0)
    lane = lax.broadcasted_iota(jnp.int32, (LANES, LANES), 1)

    rolled_ref[0] = jnp.zeros((LANES, LANES), NARROW)
    before = jnp.zeros((LANES, LANES), WIDE)
    for block in range(count):
        now = jnp.broadcast_to(taps_ref[block : block + 1, :], (LANES, LANES))
        now = pltpu.roll(now, 0, 1, stride=1, stride_axis=0)
        rolled_ref[block + 1] = jnp.where(lane >= row, now, before).astype(NARROW)
        before = now

    flip = jnp.where(lane + row == LANES - 1, 1.0, 0.0).astype(NARROW)
    for half in range(2):
        turned_ref[half * LANES : (half + 1) * LANES, :] = lax.dot_general(
            flip,
            gated_ref[:, half * LANES : (half + 1) * LANES],
            (((1,), (1,)), ((), ())),
            preferred_element_type=WIDE,
        ).astype(NARROW)

    def finish(block, now, later):
        kept = jnp.where(lane <= row, now, later)
        lag_ref[block : block + 1, :] = jnp.sum(kept, axis=0, keepdims=True)

    pending = None
    odd = None
    for step in range(pairs):
        weights = jnp.concatenate(
            [
                jnp.concatenate([rolled_ref[2 * step + 1], rolled_ref[2 * step + 2]], axis=1),
                jnp.concatenate([rolled_ref[2 * step], rolled_ref[2 * step + 1]], axis=1),
            ],
            axis=0,
        )
        offset = step * CHANNELS
        conv = jnp.dot(gated_ref[: height - offset, :], weights, preferred_element_type=WIDE)
        corr = lax.dot_general(
            scaled_ref[offset:height, :], weights, (((1,), (1,)), ((), ())), preferred_element_type=WIDE
        )
        if step == 0:
            conv_ref[...] = conv
            corr_ref[...] = corr
        else:
            conv_ref[offset:, :] += conv
            corr_ref[: height - offset, :] += corr
        depth = min(height, -(-(height - offset) // 256) * 256)
        product = jnp.dot(
            turned_ref[:, :depth], scaled_ref[offset : offset + depth, :], preferred_element_type=WIDE
        )
        even = product[:LANES, :LANES] + product[LANES:, LANES:]
        even = pltpu.roll(even, 1, 1, stride=1, stride_axis=0)
        if step > 0:
            odd = odd + product[LANES:, :LANES]
            odd = pltpu.roll(odd, 1, 1, stride=1, stride_axis=0)
            finish(2 * step - 2, pending, odd)
            finish(2 * step - 1, odd, even)
        pending = even
        odd = product[:LANES, LANES:]
    odd = pltpu.roll(odd, 1, 1, stride=1, stride_axis=0)
    finish(count - 2, pending, odd)
    finish(count - 1, odd, jnp.zeros_like(odd))

    index = lax.axis_index("ctx")
    per_row = LANES // CHANNELS
    skip = skip_ref[pl.ds(index // per_row, 1), :]
    skip = pltpu.roll(jnp.broadcast_to(skip, (LANES, LANES)), LANES - index % per_row * CHANNELS, 1)
    skip = skip.T[:CHANNELS]
    skip = jnp.concatenate([skip, skip], axis=1)

    bias = jnp.zeros((CHANNELS, 2 * LANES), WIDE)
    for pair in range(pairs):
        rows = slice(pair * CHANNELS, (pair + 1) * CHANNELS)
        gated = gated_ref[rows, :].astype(WIDE)
        scaled = scaled_ref[rows, :].astype(WIDE)
        bias = bias + gated * scaled
        conv = (conv_ref[rows, :] + skip * gated).astype(NARROW)
        corr = (corr_ref[rows, :] + skip * scaled).astype(NARROW)
        for half in range(2):
            columns = slice(half * LANES, (half + 1) * LANES)
            first = starts_back[2 * pair + half]
            out_ref[first : first + CHANNELS, :] = conv[:, columns]
            out_ref[first + CHANNELS : first + EXTRA, :] = corr[:, columns]
    bias = jnp.broadcast_to(jnp.sum(bias, axis=1, keepdims=True), (CHANNELS, LANES))
    bias = jnp.concatenate([bias] * per_row, axis=0).T[0:1]
    bias_high = bias.astype(NARROW).astype(WIDE)
    even = lax.broadcasted_iota(jnp.int32, (1, LANES), 1) // CHANNELS % 2 == 0
    tail = jnp.where(even, bias_high, bias - bias_high)
    for block in range(count):
        rows = jnp.concatenate([lag_ref[block : block + 1, :], tail], axis=0)
        out_ref[starts_back[block] + EXTRA : starts_back[block] + ROWS, :] = rows.astype(NARROW)


def finish_kernel(
    in_ref, key_ref, value_ref, grad_ref, query_out, key_out, value_out, filter_out, bias_out, held_ref, sems
):
    per_block = LANES // CHANNELS
    lane = lax.broadcasted_iota(jnp.int32, (1, LANES), 1) // CHANNELS
    starts = first_rows(filter_out.shape[0], True)
    copies = []
    for piece in range(key_ref.shape[1] // PIECE):
        for block in range(piece * PIECE // LANES, (piece + 1) * PIECE // LANES):
            columns = slice(block * LANES, (block + 1) * LANES)
            members = range(block * per_block, (block + 1) * per_block)

            def gather(offset):
                parts = [in_ref[starts[member] + offset : starts[member] + offset + CHANNELS, :] for member in members]
                return jnp.concatenate(parts, axis=0).T.astype(WIDE)

            conv, corr = gather(0), gather(CHANNELS)
            held_ref[0, :, columns] = (grad_ref[:, columns].astype(WIDE) * conv).astype(NARROW)
            held_ref[1, :, columns] = (corr * value_ref[:, columns].astype(WIDE)).astype(NARROW)
            held_ref[2, :, columns] = (corr * key_ref[:, columns].astype(WIDE)).astype(NARROW)
        columns = pl.ds(piece * PIECE, PIECE)
        for place, target in enumerate((query_out, key_out, value_out)):
            copy = pltpu.make_async_copy(
                held_ref.at[place, :, columns], target.at[:, columns], sems.at[piece, place]
            )
            copy.start()
            copies.append(copy)

    for block in range(key_ref.shape[1] // LANES):
        total = jnp.zeros((1, LANES), WIDE)
        for part in range(per_block):
            member = block * per_block + part
            rows = in_ref[starts[member] + EXTRA : starts[member] + ROWS, :].astype(WIDE)
            filter_out[member : member + 1, :] = rows[0:1]
            both = rows[1:2] + pltpu.roll(rows[1:2], CHANNELS, 1)
            total = total + jnp.where(lane == part, both, 0.0)
        bias_out[block : block + 1, :] = total
    for copy in copies:
        copy.wait()


def exchange(messages, back=False):
    count = lax.axis_size("ctx")
    split = messages.reshape(count, ROWS // 2, 2, LANES)
    moved = lax.all_to_all(
        split, "ctx", split_axis=0, concat_axis=0, tiled=True, axis_index_groups=[listing(count, back)]
    )
    return moved.reshape(messages.shape)


def on_device(query_gate, key_gate, value_branch, grad_out, filters, skip_bias):
    tokens, channels = query_gate.shape
    count = lax.axis_size("ctx")
    height = count // 2 * CHANNELS
    message = jax.ShapeDtypeStruct((count * ROWS, LANES), NARROW)
    grant = pltpu.CompilerParams(vmem_limit_bytes=16 * 1024 * 1024)
    hbm = pl.BlockSpec(memory_space=pltpu.HBM)
    vmem = pl.BlockSpec(memory_space=pltpu.VMEM)
    pieces = channels // PIECE
    sent = pl.pallas_call(
        gate_kernel,
        out_shape=message,
        in_specs=[hbm] * 5,
        out_specs=vmem,
        scratch_shapes=[
            pltpu.VMEM((4, tokens, channels), NARROW),
            pltpu.VMEM(filters.shape, WIDE),
            pltpu.SemaphoreType.DMA((pieces, 4)),
            pltpu.SemaphoreType.DMA,
        ],
        compiler_params=grant,
        name="gate",
    )(
        *(
            pltpu.with_memory_space_constraint(argument, pltpu.HBM)
            for argument in (query_gate, key_gate, value_branch, grad_out, filters)
        )
    )
    moved = exchange(sent)
    results = pl.pallas_call(
        sequence_kernel,
        out_shape=message,
        scratch_shapes=[
            pltpu.VMEM((height, 2 * LANES), NARROW),
            pltpu.VMEM((2 * height, 2 * LANES), NARROW),
            pltpu.VMEM((count, LANES), WIDE),
            pltpu.VMEM((count + 1, LANES, LANES), NARROW),
            pltpu.VMEM((2 * LANES, height), NARROW),
            pltpu.VMEM((height, 2 * LANES), WIDE),
            pltpu.VMEM((height, 2 * LANES), WIDE),
            pltpu.VMEM((count, LANES), WIDE),
        ],
        compiler_params=grant,
        name="sequence",
    )(skip_bias.reshape(channels // LANES, LANES), moved)
    back = exchange(results, True)
    wide_out = jax.ShapeDtypeStruct((tokens, channels), NARROW)
    grad_query, grad_key, grad_value, grad_filters, grad_bias = pl.pallas_call(
        finish_kernel,
        out_shape=(
            wide_out,
            wide_out,
            wide_out,
            jax.ShapeDtypeStruct(filters.shape, WIDE),
            jax.ShapeDtypeStruct((channels // LANES, LANES), WIDE),
        ),
        in_specs=[vmem] * 4,
        out_specs=(hbm, hbm, hbm, vmem, vmem),
        scratch_shapes=[
            pltpu.VMEM((3, tokens, channels), NARROW),
            pltpu.SemaphoreType.DMA((pieces, 3)),
        ],
        compiler_params=grant,
        name="finish",
    )(back, key_gate, value_branch, grad_out)
    return grad_query, grad_key, grad_value, grad_filters, grad_bias.reshape(channels)


def solution(mesh):
    in_specs = (
        P("ctx", "ch"),
        P("ctx", "ch"),
        P("ctx", "ch"),
        P("ctx", "ch"),
        P("ch", "ctx"),
        P("ch"),
    )
    out_specs = (P("ctx", "ch"), P("ctx", "ch"), P("ctx", "ch"), P("ch", "ctx"), P("ch"))
    return jax.shard_map(
        on_device, mesh=mesh, in_specs=in_specs, out_specs=out_specs, check_vma=False
    )
```

```python
import jax
import jax.numpy as jnp
from jax import lax
from jax.experimental import pallas as pl
from jax.experimental.pallas import tpu as pltpu
from jax.sharding import PartitionSpec as P

CHANNELS = 16
EXTRA = 2 * CHANNELS
ROWS = EXTRA + 2
LANES = 128
PIECE = 4 * LANES
SIDE = 4
STEP = 9
STEP_BACK = 13
WIDE = jnp.float32
NARROW = jnp.bfloat16


def listing(count, back=False):
    ring = count // SIDE
    step = STEP_BACK if back else STEP
    return [step * turn % ring * SIDE + place for place in range(SIDE) for turn in range(ring)]


def first_rows(count, back=False):
    order = listing(count, back)
    return [order.index(device) * ROWS for device in range(count)]


def gate_kernel(
    query_ref, key_ref, value_ref, grad_ref, filter_ref, out_ref, held_ref, taps_ref, sems, taps_sem
):
    per_block = LANES // CHANNELS
    pieces = query_ref.shape[1] // PIECE
    starts = first_rows(filter_ref.shape[0])
    copies = []
    for piece in range(pieces):
        columns = pl.ds(piece * PIECE, PIECE)
        copies.append(
            [
                pltpu.make_async_copy(
                    source.at[:, columns], held_ref.at[place, :, columns], sems.at[piece, place]
                )
                for place, source in enumerate((key_ref, value_ref, query_ref, grad_ref))
            ]
        )
    taps_copy = pltpu.make_async_copy(filter_ref, taps_ref, taps_sem)
    for group in copies:
        for copy in group:
            copy.start()
    taps_copy.start()

    for piece in range(pieces):
        for copy in copies[piece]:
            copy.wait()
        for block in range(piece * PIECE // LANES, (piece + 1) * PIECE // LANES):
            columns = slice(block * LANES, (block + 1) * LANES)
            key, value, query, grad = (held_ref[place, :, columns] for place in range(4))
            gated = (key * value).T
            scaled = (query * grad).T
            for part in range(per_block):
                rows = slice(part * CHANNELS, (part + 1) * CHANNELS)
                first = starts[block * per_block + part]
                out_ref[first : first + CHANNELS, :] = gated[rows]
                out_ref[first + CHANNELS : first + EXTRA, :] = scaled[rows]
    taps_copy.wait()
    for group in range(filter_ref.shape[0]):
        taps = jnp.broadcast_to(taps_ref[group : group + 1, :], (2, LANES))
        out_ref[starts[group] + EXTRA : starts[group] + ROWS, :] = taps.astype(NARROW)


def sequence_kernel(
    skip_ref, in_ref, out_ref, gated_ref, scaled_ref, taps_ref, rolled_ref, turned_ref, conv_ref, corr_ref, lag_ref
):
    count = in_ref.shape[0] // ROWS
    starts = first_rows(count)
    starts_back = first_rows(count, True)
    pairs = count // 2
    height = pairs * CHANNELS
    for block in range(count):
        rows = slice(block // 2 * CHANNELS, (block // 2 + 1) * CHANNELS)
        columns = slice(block % 2 * LANES, (block % 2 + 1) * LANES)
        first = starts[block]
        gated_ref[rows, columns] = in_ref[first : first + CHANNELS, :]
        scaled_ref[rows, columns] = in_ref[first + CHANNELS : first + EXTRA, :]
        taps_ref[block : block + 1, :] = in_ref[first + EXTRA : first + ROWS, :].astype(WIDE)[0:1]
    scaled_ref[height:, :] = jnp.zeros((height, 2 * LANES), NARROW)

    row = lax.broadcasted_iota(jnp.int32, (LANES, LANES), 0)
    lane = lax.broadcasted_iota(jnp.int32, (LANES, LANES), 1)

    rolled_ref[0] = jnp.zeros((LANES, LANES), NARROW)
    before = jnp.zeros((LANES, LANES), WIDE)
    for block in range(count):
        now = jnp.broadcast_to(taps_ref[block : block + 1, :], (LANES, LANES))
        now = pltpu.roll(now, 0, 1, stride=1, stride_axis=0)
        rolled_ref[block + 1] = jnp.where(lane >= row, now, before).astype(NARROW)
        before = now

    flip = jnp.where(lane + row == LANES - 1, 1.0, 0.0).astype(NARROW)
    for half in range(2):
        turned_ref[half * LANES : (half + 1) * LANES, :] = lax.dot_general(
            flip,
            gated_ref[:, half * LANES : (half + 1) * LANES],
            (((1,), (1,)), ((), ())),
            preferred_element_type=WIDE,
        ).astype(NARROW)

    def finish(block, now, later):
        kept = jnp.where(lane <= row, now, later)
        lag_ref[block : block + 1, :] = jnp.sum(kept, axis=0, keepdims=True)

    pending = None
    odd = None
    for step in range(pairs):
        weights = jnp.concatenate(
            [
                jnp.concatenate([rolled_ref[2 * step + 1], rolled_ref[2 * step + 2]], axis=1),
                jnp.concatenate([rolled_ref[2 * step], rolled_ref[2 * step + 1]], axis=1),
            ],
            axis=0,
        )
        offset = step * CHANNELS
        conv = jnp.dot(gated_ref[: height - offset, :], weights, preferred_element_type=WIDE)
        corr = lax.dot_general(
            scaled_ref[offset:height, :], weights, (((1,), (1,)), ((), ())), preferred_element_type=WIDE
        )
        if step == 0:
            conv_ref[...] = conv
            corr_ref[...] = corr
        else:
            conv_ref[offset:, :] += conv
            corr_ref[: height - offset, :] += corr
        depth = min(height, -(-(height - offset) // LANES) * LANES)
        product = jnp.dot(
            turned_ref[:, :depth], scaled_ref[offset : offset + depth, :], preferred_element_type=WIDE
        )
        even = product[:LANES, :LANES] + product[LANES:, LANES:]
        even = pltpu.roll(even, 1, 1, stride=1, stride_axis=0)
        if step > 0:
            odd = odd + product[LANES:, :LANES]
            odd = pltpu.roll(odd, 1, 1, stride=1, stride_axis=0)
            finish(2 * step - 2, pending, odd)
            finish(2 * step - 1, odd, even)
        pending = even
        odd = product[:LANES, LANES:]
    odd = pltpu.roll(odd, 1, 1, stride=1, stride_axis=0)
    finish(count - 2, pending, odd)
    finish(count - 1, odd, jnp.zeros_like(odd))

    index = lax.axis_index("ctx")
    per_row = LANES // CHANNELS
    skip = skip_ref[pl.ds(index // per_row, 1), :]
    skip = pltpu.roll(jnp.broadcast_to(skip, (LANES, LANES)), LANES - index % per_row * CHANNELS, 1)
    skip = skip.T[:CHANNELS]
    skip = jnp.concatenate([skip, skip], axis=1)

    bias = jnp.zeros((CHANNELS, 2 * LANES), WIDE)
    for pair in range(pairs):
        rows = slice(pair * CHANNELS, (pair + 1) * CHANNELS)
        gated = gated_ref[rows, :].astype(WIDE)
        scaled = scaled_ref[rows, :].astype(WIDE)
        bias = bias + gated * scaled
        conv = (conv_ref[rows, :] + skip * gated).astype(NARROW)
        corr = (corr_ref[rows, :] + skip * scaled).astype(NARROW)
        for half in range(2):
            columns = slice(half * LANES, (half + 1) * LANES)
            first = starts_back[2 * pair + half]
            out_ref[first : first + CHANNELS, :] = conv[:, columns]
            out_ref[first + CHANNELS : first + EXTRA, :] = corr[:, columns]
    bias = jnp.broadcast_to(jnp.sum(bias, axis=1, keepdims=True), (CHANNELS, LANES))
    bias = jnp.concatenate([bias] * per_row, axis=0).T[0:1]
    bias_high = bias.astype(NARROW).astype(WIDE)
    even = lax.broadcasted_iota(jnp.int32, (1, LANES), 1) // CHANNELS % 2 == 0
    tail = jnp.where(even, bias_high, bias - bias_high)
    for block in range(count):
        rows = jnp.concatenate([lag_ref[block : block + 1, :], tail], axis=0)
        out_ref[starts_back[block] + EXTRA : starts_back[block] + ROWS, :] = rows.astype(NARROW)


def finish_kernel(
    in_ref, key_ref, value_ref, grad_ref, query_out, key_out, value_out, filter_out, bias_out, held_ref, sems
):
    per_block = LANES // CHANNELS
    lane = lax.broadcasted_iota(jnp.int32, (1, LANES), 1) // CHANNELS
    starts = first_rows(filter_out.shape[0], True)
    copies = []
    for piece in range(key_ref.shape[1] // PIECE):
        for block in range(piece * PIECE // LANES, (piece + 1) * PIECE // LANES):
            columns = slice(block * LANES, (block + 1) * LANES)
            members = range(block * per_block, (block + 1) * per_block)

            def gather(offset):
                parts = [in_ref[starts[member] + offset : starts[member] + offset + CHANNELS, :] for member in members]
                return jnp.concatenate(parts, axis=0).T.astype(WIDE)

            conv, corr = gather(0), gather(CHANNELS)
            held_ref[0, :, columns] = (grad_ref[:, columns].astype(WIDE) * conv).astype(NARROW)
            held_ref[1, :, columns] = (corr * value_ref[:, columns].astype(WIDE)).astype(NARROW)
            held_ref[2, :, columns] = (corr * key_ref[:, columns].astype(WIDE)).astype(NARROW)
        columns = pl.ds(piece * PIECE, PIECE)
        for place, target in enumerate((query_out, key_out, value_out)):
            copy = pltpu.make_async_copy(
                held_ref.at[place, :, columns], target.at[:, columns], sems.at[piece, place]
            )
            copy.start()
            copies.append(copy)

    for block in range(key_ref.shape[1] // LANES):
        total = jnp.zeros((1, LANES), WIDE)
        for part in range(per_block):
            member = block * per_block + part
            rows = in_ref[starts[member] + EXTRA : starts[member] + ROWS, :].astype(WIDE)
            filter_out[member : member + 1, :] = rows[0:1]
            both = rows[1:2] + pltpu.roll(rows[1:2], CHANNELS, 1)
            total = total + jnp.where(lane == part, both, 0.0)
        bias_out[block : block + 1, :] = total
    for copy in copies:
        copy.wait()


def exchange(messages, back=False):
    count = lax.axis_size("ctx")
    split = messages.reshape(count, ROWS // 2, 2, LANES)
    moved = lax.all_to_all(
        split, "ctx", split_axis=0, concat_axis=0, tiled=True, axis_index_groups=[listing(count, back)]
    )
    return moved.reshape(messages.shape)


def on_device(query_gate, key_gate, value_branch, grad_out, filters, skip_bias):
    tokens, channels = query_gate.shape
    count = lax.axis_size("ctx")
    height = count // 2 * CHANNELS
    message = jax.ShapeDtypeStruct((count * ROWS, LANES), NARROW)
    grant = pltpu.CompilerParams(vmem_limit_bytes=16 * 1024 * 1024)
    hbm = pl.BlockSpec(memory_space=pltpu.HBM)
    vmem = pl.BlockSpec(memory_space=pltpu.VMEM)
    pieces = channels // PIECE
    sent = pl.pallas_call(
        gate_kernel,
        out_shape=message,
        in_specs=[hbm] * 5,
        out_specs=vmem,
        scratch_shapes=[
            pltpu.VMEM((4, tokens, channels), NARROW),
            pltpu.VMEM(filters.shape, WIDE),
            pltpu.SemaphoreType.DMA((pieces, 4)),
            pltpu.SemaphoreType.DMA,
        ],
        compiler_params=grant,
        name="gate",
    )(
        *(
            pltpu.with_memory_space_constraint(argument, pltpu.HBM)
            for argument in (query_gate, key_gate, value_branch, grad_out, filters)
        )
    )
    moved = exchange(sent)
    results = pl.pallas_call(
        sequence_kernel,
        out_shape=message,
        scratch_shapes=[
            pltpu.VMEM((height, 2 * LANES), NARROW),
            pltpu.VMEM((2 * height, 2 * LANES), NARROW),
            pltpu.VMEM((count, LANES), WIDE),
            pltpu.VMEM((count + 1, LANES, LANES), NARROW),
            pltpu.VMEM((2 * LANES, height), NARROW),
            pltpu.VMEM((height, 2 * LANES), WIDE),
            pltpu.VMEM((height, 2 * LANES), WIDE),
            pltpu.VMEM((count, LANES), WIDE),
        ],
        compiler_params=grant,
        name="sequence",
    )(skip_bias.reshape(channels // LANES, LANES), moved)
    back = exchange(results, True)
    wide_out = jax.ShapeDtypeStruct((tokens, channels), NARROW)
    grad_query, grad_key, grad_value, grad_filters, grad_bias = pl.pallas_call(
        finish_kernel,
        out_shape=(
            wide_out,
            wide_out,
            wide_out,
            jax.ShapeDtypeStruct(filters.shape, WIDE),
            jax.ShapeDtypeStruct((channels // LANES, LANES), WIDE),
        ),
        in_specs=[vmem] * 4,
        out_specs=(hbm, hbm, hbm, vmem, vmem),
        scratch_shapes=[
            pltpu.VMEM((3, tokens, channels), NARROW),
            pltpu.SemaphoreType.DMA((pieces, 3)),
        ],
        compiler_params=grant,
        name="finish",
    )(back, key_gate, value_branch, grad_out)
    return grad_query, grad_key, grad_value, grad_filters, grad_bias.reshape(channels)


def solution(mesh):
    in_specs = (
        P("ctx", "ch"),
        P("ctx", "ch"),
        P("ctx", "ch"),
        P("ctx", "ch"),
        P("ch", "ctx"),
        P("ch"),
    )
    out_specs = (P("ctx", "ch"), P("ctx", "ch"), P("ctx", "ch"), P("ch", "ctx"), P("ch"))
    return jax.shard_map(
        on_device, mesh=mesh, in_specs=in_specs, out_specs=out_specs, check_vma=False
    )
```
